512 devices in a mesh: dp: 32 (over z, core), expert: 16 (over x, y).
Axes of the slice: x: 4, y: 4, z: 16, core: 2. Of those that a mesh axis runs over, the one named last changes fastest.
Arguments:
- acts: bfloat16 [16384, 16, 2048], P('dp', 'expert'), may hold values from -6 to 6
- grads: bfloat16 [16384, 16, 384], P('dp', 'expert'), may hold values from -0.046875 to 0.046875
- tile_expert: int32 [64, 16, 1], P('dp', 'expert'), may hold values from 0 to 1
- momentum: float32 [2048, 32, 384], P('dp', 'expert'), may hold values from -48 to 48
- packing: int32 [32, 1], replicated, may hold values from 0 to 15; in each aligned block of 32 rows (0 to 31, 32 to 63, ...) at most 4 rows name the same one
Outputs:
- new_momentum: float32 [2048, 32, 384], P('dp', 'expert')
- stacked_update: bfloat16 [2048, 64, 384], P('dp', 'expert')
The draws below stay inside these ranges and needn't reach their ends.
Inputs may be any that keep to these rules, and one draw needn't show every extreme that they name: `tile_expert`: local expert index within the tile's group. `packing`: at most 4 experts share an owner, and some owner holds exactly 4.
All inputs are finite; a program needn't handle non-finite values.
Results may differ from the reference program's by a relative error of at most 0.04.
Values may be sent and summed in bfloat16 or wider, within the bound.
No kernel may reach another device: no remote copies, remote signals or barrier semaphores. Data moves between devices by JAX's collectives and lax.ppermute only.
A program may use at most 64 MiB of HBM per device.

```python
import math
import jax
import jax.numpy as jnp
import numpy as np
from jax import lax

D = 2048
FF = 384
TILE = 256
TILES_DEV = 2
EXP_GRP = 2
ITERS = 3
MOST = 4
ROWS = 16384
TILES = 64
GROUPS = 16
EXPERTS = 32
SLOTS = 64
N_DP = 32


def draw_momentum(key, part):
    key = jax.random.fold_in(key, 5)
    position = jnp.arange(D, dtype=jnp.float32) / D
    scale = 0.5 * jnp.exp(jnp.log(16.0) * position)
    base = jnp.clip(jax.random.normal(key, (D, EXPERTS, FF), jnp.float32), -6.0, 6.0)
    return base * scale[:, None, None]


def steps_of(stream_key, dims, cuts, least, top_value):
    loudness, own = 1.0, jax.random.fold_in(stream_key, 6)
    for axis_at, parts in cuts:
        draws = jnp.exp(jax.random.uniform(jax.random.fold_in(own, axis_at), (parts,), jnp.float32, least / len(cuts), top_value / len(cuts)))
        loudness = loudness * jnp.repeat(draws, dims[axis_at] // parts).reshape([-1 if axis == axis_at else 1 for axis in range(len(dims))])
    return loudness


def picks_of(own_key, rows, count, top, lift):
    order = jax.random.permutation(jax.random.fold_in(own_key, 1), count)
    pull = order
    for power in range(3):
        pull = pull * pull // count
    pull = pull * lift // count
    tickets = jax.random.randint(jax.random.fold_in(own_key, 2), (rows, count), 0, 4096) + pull
    fixed_rows = jax.random.permutation(jax.random.fold_in(own_key, 3), rows)[jnp.arange(count) % rows]
    tickets = jnp.where(jnp.arange(rows)[:, None] == fixed_rows[None, :], 1 << 14, tickets)
    merit = tickets * count + jnp.arange(count)
    return lax.top_k(merit.astype(jnp.int32), top)[1].astype(jnp.int32)


def deal_out(rng, own, number, rows, count, top, limit, slope):
    ranking = jax.random.permutation(rng, count)
    crowded, usual = portions_of(count, rows * top, limit, slope, True), portions_of(count, rows * top, limit, slope, False)
    places = jnp.arange(count)

    def named(lengths, turn):
        used = int((lengths > 0).sum())
        fixed = max(1, used // 4)
        shifted = fixed + (places - fixed + turn * (used - fixed)) % max(1, count - fixed)
        return jnp.zeros((count,), jnp.int32).at[ranking[jnp.where(places < fixed, places, shifted)]].set(jnp.asarray(lengths, jnp.int32))

    lengths = jnp.where(number % 4 == 0, named(crowded, number // 4), named(usual, number - number // 4 - 1))
    mixed = jax.random.permutation(jax.random.fold_in(own, 3), count)
    giver, taker = mixed[0:count // 2 * 2:2], mixed[1:count // 2 * 2:2]
    slack = jnp.minimum(lengths[giver] - 1, limit - lengths[taker]) // 2
    slack = jnp.where((giver == ranking[0]) | (taker == ranking[0]) | (lengths[taker] == 0), 0, jnp.maximum(slack, 0))
    shifted = jax.random.randint(jax.random.fold_in(own, 4), (count // 2,), 0, 1 << 20) % (slack + 1)
    lengths = lengths.at[giver].add(-shifted).at[taker].add(shifted)
    members = jnp.searchsorted(jnp.cumsum(lengths), jnp.arange(rows * top), side="right").astype(jnp.int32)
    table = members.reshape(top, rows).T
    table = table[jax.random.permutation(jax.random.fold_in(own, 1), rows)]
    turn = jax.random.randint(jax.random.fold_in(own, 2), (rows, 1), 0, top)
    return jnp.take_along_axis(table, (jnp.arange(top)[None, :] + turn) % top, axis=1)


def portions_of(count, total, limit, skew, full):
    portions = [(1 << 20) // math.isqrt(rank ** skew) + 1 for rank in range(1, count + 1)]
    largest = limit if full else min(limit, max(-(-total // count), total * portions[0] // sum(portions)))
    least = 1 if total - largest >= count - 1 else 0
    given, spare = [largest] + [least] * (count - 1), total - largest - least * (count - 1)
    while spare > 0:
        free = [i for i in range(1, count) if given[i] < largest] or [i for i in range(1, count) if given[i] < limit]
        mass, budget = sum([portions[i] for i in free]), spare
        for i in free:
            more = min(limit - given[i], max(1, budget * portions[i] // mass), spare)
            given[i] = given[i] + more
            spare = spare - more
    return np.array(given)


def gaussian(own_key, extent, scale, bound, cuts=(), held_as=jnp.bfloat16):
    loudness = steps_of(own_key, extent, cuts, -0.22, 0.18) if cuts else 1.0
    array = jax.random.normal(own_key, extent, jnp.float32) * scale * loudness
    return jnp.minimum(jnp.maximum(array, -bound), bound).astype(held_as)


def setup_inputs(seed: int = 0) -> dict:
    key_of = jax.random.split(jax.random.key(seed), 6)
    acts = gaussian(key_of[0], (ROWS, GROUPS, D), 1.0, 6.0, ((0, 32), (1, 16)))
    grads = gaussian(key_of[1], (ROWS, GROUPS, FF), ROWS ** -0.5, 0.046875, ((0, 32), (1, 16)))
    tile_expert = picks_of(key_of[2], TILES * GROUPS, EXP_GRP, 1, 4096).reshape((TILES, GROUPS, 1))
    momentum = draw_momentum(jax.random.fold_in(key_of[5], 71), 0)
    packing_keys = jax.random.split(jax.random.fold_in(key_of[4], 1), EXPERTS // EXPERTS)
    packing_turns = jax.random.permutation(jax.random.fold_in(key_of[4], 3), EXPERTS // EXPERTS)
    packing = jax.vmap(lambda own, number: deal_out(jax.random.fold_in(key_of[4], 2), own, number, EXPERTS, GROUPS, 1, MOST, 2))(packing_keys, packing_turns).reshape((EXPERTS, 1))
    return {"acts": acts, "grads": grads, "tile_expert": tile_expert, "momentum": momentum, "packing": packing}


COEF_A = 3.4445
COEF_B = -4.775
COEF_C = 2.0315
BETA = 0.95
EPSILON = 1e-07

def shard_partial(acts_shard, grads_shard, expert_ids):
    summed = jnp.zeros((EXP_GRP, D, FF), jnp.float32)
    for tile_pos in range(TILES_DEV):
        contrib = jnp.dot(acts_shard[tile_pos].T, grads_shard[tile_pos], preferred_element_type=jnp.float32)
        onehot = (expert_ids[tile_pos] == jnp.arange(EXP_GRP, dtype=jnp.int32)).astype(jnp.float32)
        summed = summed + onehot[:, None, None] * contrib[None]
    rounded = lax.optimization_barrier(summed.astype(jnp.bfloat16))
    return rounded.astype(jnp.float32)

def group_gradient(inputs):
    acts_group, grads_group, ids_group = inputs
    acts_tiles = acts_group.reshape(N_DP, TILES_DEV, TILE, D)
    grads_tiles = grads_group.reshape(N_DP, TILES_DEV, TILE, FF)
    ids_tiles = ids_group.reshape(N_DP, TILES_DEV)

    def accumulate(running, shard):
        return (running + shard_partial(shard[0], shard[1], shard[2]), None)
    summed, unused = lax.scan(accumulate, jnp.zeros((EXP_GRP, D, FF), jnp.float32), (acts_tiles, grads_tiles, ids_tiles))
    return summed

def gram_matrix(current):
    pieces = current.astype(jnp.float32).reshape(N_DP, D // N_DP, FF)
    partial_value = jnp.einsum('idf,idg->ifg', pieces, pieces)
    rounded = lax.optimization_barrier(partial_value.astype(jnp.bfloat16))
    return lax.optimization_barrier(jnp.sum(rounded.astype(jnp.float32), axis=0))

def orthogonal_one(block):
    gram0 = gram_matrix(block)
    inv_norm = 1.0 / (jnp.sqrt(jnp.trace(gram0)) + EPSILON)
    current = (block.astype(jnp.float32) * inv_norm).astype(jnp.bfloat16)
    weights_a = (gram0 * (inv_norm * inv_norm)).astype(jnp.bfloat16)
    result = current
    for sweep in range(ITERS):
        if sweep > 0:
            weights_a = gram_matrix(current).astype(jnp.bfloat16)
        times_a = jnp.dot(current, weights_a, preferred_element_type=jnp.float32)
        times_aa = jnp.dot(times_a.astype(jnp.bfloat16), weights_a, preferred_element_type=jnp.float32)
        combined = COEF_A * current.astype(jnp.float32) + COEF_B * times_a + COEF_C * times_aa
        if sweep < ITERS - 1:
            current = combined.astype(jnp.bfloat16)
        else:
            result = (combined * math.sqrt(D)).astype(jnp.bfloat16)
    return result

def reference(acts, grads, tile_expert, momentum, packing):
    grouped = lax.map(group_gradient, (jnp.moveaxis(acts, 1, 0), jnp.moveaxis(grads, 1, 0), jnp.moveaxis(tile_expert[:, :, 0], 1, 0)))
    grad = grouped.reshape(EXPERTS, D, FF).transpose(1, 0, 2)
    new_momentum = BETA * momentum + grad
    ns_input = (grad + BETA * new_momentum).astype(jnp.bfloat16)
    updates = lax.map(orthogonal_one, ns_input.transpose(1, 0, 2))
    owner_ids = packing[:, 0]
    positions = jnp.arange(EXPERTS, dtype=jnp.int32)
    shared = (owner_ids[:, None] == owner_ids[None, :]) & (positions[None, :] < positions[:, None])
    slot_rank = lax.optimization_barrier(jnp.sum(shared.astype(jnp.int32), axis=1))
    target = owner_ids * MOST + slot_rank
    stacked = jnp.zeros((SLOTS, D, FF), jnp.bfloat16).at[target].set(updates)
    return (new_momentum, stacked.transpose(1, 0, 2))
```

```python
import math

import jax
import jax.numpy as jnp
from jax import lax
from jax.experimental import pallas as pl
from jax.experimental.pallas import tpu as pltpu
from jax.sharding import PartitionSpec as P

D = 2048
FF = 384
TILE = 256
ITERS = 3
MOST = 4
CORES = 2
NEAR = 4
LANE = 128

COEF_A = 3.4445
COEF_B = -4.775
COEF_C = 2.0315
BETA = 0.95
EPSILON = 1e-07
BLOCKS = ((0, 0), (0, 1), (0, 2), (1, 1), (1, 2), (2, 2))


def split(x):
    high = x.astype(jnp.bfloat16)
    return high, (x - high.astype(jnp.float32)).astype(jnp.bfloat16)


def dot(x, y):
    return jnp.dot(x, y, preferred_element_type=jnp.float32)


def dot3(x, y):
    (xh, xl), (yh, yl) = x, y
    return dot(xh, yh) + (dot(xh, yl) + dot(xl, yh))


def newton_schulz_kernel(gram_ref, x_ref, out_ref):
    blocks = {}
    for at, (i, j) in enumerate(BLOCKS):
        block = gram_ref[at * LANE : (at + 1) * LANE, :]
        blocks[i, j] = block
        if i != j:
            blocks[j, i] = block.T
    gram = jnp.concatenate(
        [jnp.concatenate([blocks[i, j] for j in range(3)], axis=1) for i in range(3)], axis=0
    )
    rows = lax.broadcasted_iota(jnp.int32, (FF, FF), 0)
    cols = lax.broadcasted_iota(jnp.int32, (FF, FF), 1)
    eye = (rows == cols).astype(jnp.float32)
    trace = jnp.sum(jnp.sum(gram * eye, axis=1, keepdims=True), axis=0, keepdims=True)
    inv_norm = 1.0 / (jnp.sqrt(trace) + EPSILON)
    weights = gram * (inv_norm * inv_norm)
    total = None
    for sweep in range(ITERS):
        parts = split(weights)
        poly = COEF_A * eye + COEF_B * weights + COEF_C * dot3(parts, parts)
        poly_parts = split(poly)
        total = poly if total is None else dot3(split(total), poly_parts)
        if sweep < ITERS - 1:
            weights = dot3(split(dot3(parts, poly_parts)), poly_parts)
    high, low = split(total * (inv_norm * math.sqrt(D)))
    x = x_ref[...]
    out_ref[...] = (dot(x, high) + dot(x, low)).astype(jnp.bfloat16)


def body(acts, grads, tile_expert, momentum, packing):
    n_dp = lax.axis_size("dp")
    n_z = n_dp // CORES
    far = n_z // NEAR
    local_rows = momentum.shape[0]
    pair_rows = CORES * local_rows
    core = lax.rem(lax.axis_index("dp"), CORES)
    swap = [(i, i ^ 1) for i in range(n_dp)]
    near_groups = [
        [(b * NEAR + j) * CORES + c for j in range(NEAR)] for b in range(far) for c in range(CORES)
    ]
    far_groups = [
        [(j * NEAR + b) * CORES + c for j in range(far)] for b in range(NEAR) for c in range(CORES)
    ]
    z_groups = [[j * CORES + c for j in range(n_z)] for c in range(CORES)]

    flat_acts = acts[:, 0, :]
    flat_grads = grads[:, 0, :]
    row_expert = jnp.repeat(tile_expert[:, 0, 0], TILE)[:, None]

    def partial_of(expert):
        masked = jnp.where(row_expert == expert, flat_grads, jnp.zeros_like(flat_grads))
        return lax.dot_general(
            flat_acts, masked, (((0,), (0,)), ((), ())), preferred_element_type=jnp.float32
        ).astype(jnp.bfloat16)

    other = lax.ppermute(partial_of(1 - core), "dp", swap)
    chip = (partial_of(core).astype(jnp.float32) + other.astype(jnp.float32)).astype(jnp.bfloat16)
    chip = chip.reshape(far, NEAR, pair_rows, FF).transpose(1, 0, 2, 3)
    near = lax.all_to_all(chip, "dp", 0, 0, axis_index_groups=near_groups)
    near = jnp.sum(near.astype(jnp.float32), axis=0).astype(jnp.bfloat16)
    grad = lax.all_to_all(near, "dp", 0, 0, axis_index_groups=far_groups)
    grad = jnp.sum(grad.astype(jnp.float32), axis=0)

    def by_row(mine, theirs):
        low = jnp.where(core == 0, mine, theirs)
        high = jnp.where(core == 0, theirs, mine)
        return jnp.concatenate([low, high], axis=0)

    def swap_rows(value):
        halves = value.reshape(CORES, local_rows, FF)
        mine = lax.dynamic_index_in_dim(halves, core, 0, keepdims=False)
        given = lax.dynamic_index_in_dim(halves, 1 - core, 0, keepdims=False)
        theirs = lax.ppermute(given, "dp", swap)
        return jnp.where(core == 0, mine, theirs), jnp.where(core == 0, theirs, mine)

    kept = lax.dynamic_index_in_dim(momentum, core, 1, keepdims=False)
    lent = lax.dynamic_index_in_dim(momentum, 1 - core, 1, keepdims=False)
    pair_momentum = by_row(kept, lax.ppermute(lent, "dp", swap))
    pair_new = BETA * pair_momentum + grad
    ns_input = (grad + BETA * pair_new).astype(jnp.bfloat16)
    new_momentum = jnp.stack(swap_rows(pair_new), axis=1)

    gram = lax.dot_general(
        ns_input, ns_input, (((0,), (0,)), ((), ())), preferred_element_type=jnp.float32
    ).astype(jnp.bfloat16)
    packed = jnp.concatenate(
        [gram[i * LANE : (i + 1) * LANE, j * LANE : (j + 1) * LANE] for i, j in BLOCKS], axis=0
    )
    packed = packed.reshape(n_z, -1, LANE)
    piece = lax.all_to_all(packed, "dp", 0, 0, axis_index_groups=z_groups)
    piece = jnp.sum(piece.astype(jnp.float32), axis=0)
    whole = lax.all_to_all(
        jnp.broadcast_to(piece[None], packed.shape), "dp", 0, 0, axis_index_groups=z_groups
    ).reshape(-1, LANE)

    update = pl.pallas_call(
        newton_schulz_kernel,
        out_shape=jax.ShapeDtypeStruct((pair_rows, FF), jnp.bfloat16),
        in_specs=[pl.BlockSpec(memory_space=pltpu.VMEM)] * 2,
        out_specs=pl.BlockSpec(memory_space=pltpu.VMEM),
        compiler_params=pltpu.CompilerParams(vmem_limit_bytes=32 * 1024 * 1024),
    )(whole, ns_input)
    update = jnp.stack(swap_rows(update), axis=0)

    owner_ids = packing[:, 0]
    n_owner = lax.axis_size("expert")
    all_experts = owner_ids.shape[0]
    exp_count = momentum.shape[1]
    positions = jnp.arange(all_experts, dtype=jnp.int32)
    shared = (owner_ids[:, None] == owner_ids[None, :]) & (positions[None, :] < positions[:, None])
    target = owner_ids * MOST + jnp.sum(shared.astype(jnp.int32), axis=1)
    group = lax.axis_index("expert")
    my_owners = lax.dynamic_slice_in_dim(owner_ids, group * exp_count, exp_count, 0)
    goes = jnp.arange(n_owner, dtype=jnp.int32)[:, None] == my_owners[None, :]
    sent = jnp.where(goes[:, :, None, None], update[None], jnp.zeros_like(update)[None])
    got = lax.all_to_all(sent, "expert", 0, 0).reshape(all_experts, local_rows, FF)
    wanted = group * MOST + jnp.arange(MOST, dtype=jnp.int32)
    hits = target[None, :] == wanted[:, None]
    source = jnp.argmax(hits, axis=1)
    filled = jnp.any(hits, axis=1)
    slots = [
        jnp.where(
            filled[s], lax.dynamic_index_in_dim(got, source[s], 0, keepdims=False), jnp.bfloat16(0)
        )
        for s in range(MOST)
    ]
    return new_momentum, jnp.stack(slots, axis=1)


def solution(mesh):
    in_specs = (
        P("dp", "expert", None),
        P("dp", "expert", None),
        P("dp", "expert", None),
        P("dp", "expert", None),
        P(),
    )
    out_specs = (P("dp", "expert", None), P("dp", "expert", None))
    return jax.shard_map(body, mesh=mesh, in_specs=in_specs, out_specs=out_specs, check_vma=False)
```

```python
import functools
import math

import jax
import jax.numpy as jnp
import numpy as np
from jax import lax
from jax.experimental import pallas as pl
from jax.experimental.pallas import tpu as pltpu
from jax.sharding import Mesh
from jax.sharding import PartitionSpec as P

D = 2048
FF = 384
TILE = 256
ITERS = 3
MOST = 4
CORES = 2
NEAR = 4
FAR = 4
ROWS = 64
PAIR = CORES * ROWS
LANE = 128

COEF_A = 3.4445
COEF_B = -4.775
COEF_C = 2.0315
BETA = 0.95
EPSILON = 1e-07
BLOCKS = ((0, 0), (0, 1), (0, 2), (1, 1), (1, 2), (2, 2))
MIB = 1024 * 1024
VMEM = pl.BlockSpec(memory_space=pltpu.VMEM)
SMEM = pl.BlockSpec(memory_space=pltpu.SMEM)
BF16 = jnp.bfloat16
F32 = jnp.float32


def call(kernel, outs, *args, scalars=1, scratch=(), flops=0):
    many = isinstance(outs, list)
    nbytes = sum(a.size * a.dtype.itemsize for a in args)
    return pl.pallas_call(
        kernel,
        out_shape=outs,
        in_specs=[SMEM] * scalars + [VMEM] * (len(args) - scalars),
        out_specs=[VMEM] * len(outs) if many else VMEM,
        scratch_shapes=list(scratch),
        compiler_params=pltpu.CompilerParams(vmem_limit_bytes=16 * MIB),
        cost_estimate=pl.CostEstimate(flops=flops, bytes_accessed=nbytes, transcendentals=0),
    )(*args)


def shape(dims, dtype=BF16):
    return jax.ShapeDtypeStruct(dims, dtype)


def transposed_dot(x, y):
    return lax.dot_general(x, y, (((0,), (0,)), ((), ())), preferred_element_type=F32)


def partial_kernel(theirs, where_ref, acts_ref, grads_ref, out_ref, masked_ref):
    z, core = where_ref[0], where_ref[1]
    expert = 1 - core if theirs else core
    for tile in range(acts_ref.shape[0] // TILE):
        rows = slice(tile * TILE, (tile + 1) * TILE)
        factor = jnp.where(where_ref[2 + tile] == expert, 1.0, 0.0).astype(F32)
        masked_ref[rows, :] = (grads_ref[rows, :].astype(F32) * factor).astype(BF16)
    masked = masked_ref[...]
    for rel in range(NEAR):
        cls = lax.rem(z + rel, NEAR)
        for q in range(FAR):
            start = pl.multiple_of((q * NEAR + cls) * PAIR, PAIR)
            block = transposed_dot(acts_ref[:, pl.ds(start, PAIR)], masked)
            out_ref[rel, q] = block.astype(BF16)


def add_kernel(mine_ref, other_ref, own_ref, up1_ref, up2_ref, down2_ref, down1_ref):
    def total(rel, qs):
        return (mine_ref[rel, qs].astype(F32) + other_ref[rel, qs].astype(F32)).astype(BF16)

    half = FAR // 2
    own_ref[...] = total(0, slice(None))
    up1_ref[...] = total(1, slice(None))
    up2_ref[...] = total(2, slice(0, half))
    down2_ref[...] = total(2, slice(half, FAR))
    down1_ref[...] = total(3, slice(None))


def near_kernel(
    where_ref, own_ref, a_ref, b_ref, c_ref, d_ref, keep_ref, up1_ref, up2_ref, down1_ref
):
    at = where_ref[0] // NEAR
    half = FAR // 2

    def total(q):
        return own_ref[q].astype(F32) + a_ref[q].astype(F32) + b_ref[q].astype(F32)

    for rel, out_ref in enumerate((keep_ref, up1_ref, up2_ref, down1_ref)):
        q = lax.rem(at + rel, FAR)

        @pl.when(q < half)
        def _():
            out_ref[...] = (total(q) + c_ref[q].astype(F32)).astype(out_ref.dtype)

        @pl.when(q >= half)
        def _():
            out_ref[...] = (total(q) + d_ref[q - half].astype(F32)).astype(out_ref.dtype)


def momentum_kernel(
    where_ref, keep_ref, a_ref, b_ref, c_ref, kept_ref, lent_ref, ns_ref, mine_ref, give_ref, gram_ref
):
    core = where_ref[1]
    for who, old_ref, new_ref in ((core, kept_ref, mine_ref), (1 - core, lent_ref, give_ref)):
        rows = pl.ds(pl.multiple_of(who * ROWS, ROWS), ROWS)
        grad = keep_ref[rows, :] + a_ref[rows, :].astype(F32)
        grad = grad + b_ref[rows, :].astype(F32) + c_ref[rows, :].astype(F32)
        new = BETA * old_ref[...] + grad
        new_ref[...] = new
        ns_ref[rows, :] = (grad + BETA * new).astype(BF16)
    x = ns_ref[...]
    gram = transposed_dot(x, x).astype(BF16)
    for at, (i, j) in enumerate(BLOCKS):
        gram_ref[at * LANE : (at + 1) * LANE, :] = gram[
            i * LANE : (i + 1) * LANE, j * LANE : (j + 1) * LANE
        ]


def piece_kernel(parts_ref, out_ref):
    total = parts_ref[0].astype(F32)
    for at in range(1, parts_ref.shape[0]):
        total = total + parts_ref[at].astype(F32)
    for at in range(out_ref.shape[0]):
        out_ref[at] = total


def split(x):
    high = x.astype(BF16)
    return high, (x - high.astype(F32)).astype(BF16)


def dot(x, y):
    return jnp.dot(x, y, preferred_element_type=F32)


def dot3(x, y):
    (xh, xl), (yh, yl) = x, y
    return dot(xh, yh) + (dot(xh, yl) + dot(xl, yh))


def newton_schulz_kernel(owner_ref, gram_ref, x_ref, out_ref):
    blocks = {}
    for at, (i, j) in enumerate(BLOCKS):
        block = gram_ref[at * LANE : (at + 1) * LANE, :]
        blocks[i, j] = block
        if i != j:
            blocks[j, i] = block.T
    gram = jnp.concatenate(
        [jnp.concatenate([blocks[i, j] for j in range(3)], axis=1) for i in range(3)], axis=0
    )
    rows = lax.broadcasted_iota(jnp.int32, (FF, FF), 0)
    cols = lax.broadcasted_iota(jnp.int32, (FF, FF), 1)
    eye = (rows == cols).astype(F32)
    trace = jnp.sum(jnp.sum(gram * eye, axis=1, keepdims=True), axis=0, keepdims=True)
    inv_norm = 1.0 / (jnp.sqrt(trace) + EPSILON)
    weights = gram * (inv_norm * inv_norm)
    total = None
    for sweep in range(ITERS):
        parts = split(weights)
        poly = COEF_A * eye + COEF_B * weights + COEF_C * dot3(parts, parts)
        poly_parts = split(poly)
        total = poly if total is None else dot3(split(total), poly_parts)
        if sweep < ITERS - 1:
            weights = dot3(split(dot3(parts, poly_parts)), poly_parts)
    high, low = split(total * (inv_norm * math.sqrt(D)))
    x = x_ref[...]
    update = (dot(x, high) + dot(x, low)).astype(BF16)
    out_ref[...] = jnp.zeros_like(out_ref)
    for core in range(CORES):
        out_ref[core, owner_ref[0]] = update[core * ROWS : (core + 1) * ROWS, :]


def stack_kernel(source_ref, got_ref, out_ref, wide_ref):
    for slot in range(MOST):
        source = source_ref[slot]
        filled = jnp.where(source >= 0, 1.0, 0.0).astype(F32)
        wide_ref[:, slot, :] = got_ref[jnp.maximum(source, 0)].astype(F32) * filled
    out_ref[...] = wide_ref[...].astype(BF16)


def ring(size, step):
    return [(i, (i + step) % size) for i in range(size)]


def body(acts, grads, tile_expert, momentum, packing):
    z, core, group = lax.axis_index("z"), lax.axis_index("core"), lax.axis_index("expert")
    n_z, n_owner = lax.axis_size("z"), lax.axis_size("expert")
    where = jnp.concatenate([jnp.stack([z, core]), tile_expert[:, 0, 0]]).astype(jnp.int32)
    flat_acts, flat_grads = acts[:, 0, :], grads[:, 0, :]

    def go(value, step):
        return lax.ppermute(value, "z", ring(n_z, step))

    def swap(value):
        return lax.ppermute(value, "core", ring(CORES, 1))

    def partial_of(theirs):
        return call(
            functools.partial(partial_kernel, theirs),
            shape((NEAR, FAR, PAIR, FF)),
            where,
            flat_acts,
            flat_grads,
            scratch=[pltpu.VMEM(flat_grads.shape, BF16)],
            flops=2 * flat_acts.size * FF,
        )

    other = swap(partial_of(True))
    mine = partial_of(False)
    whole, half = shape((FAR, PAIR, FF)), shape((FAR // 2, PAIR, FF))
    own, up1, up2, down2, down1 = call(
        add_kernel, [whole, whole, half, half, whole], mine, other, scalars=0
    )
    chunk = shape((PAIR, FF))
    keep, up1, up2, down1 = call(
        near_kernel,
        [shape((PAIR, FF), F32), chunk, chunk, chunk],
        where,
        own,
        go(up1, 1),
        go(down1, -1),
        go(up2, 2),
        go(down2, -2),
    )
    kept = lax.dynamic_index_in_dim(momentum, core, 1, keepdims=False)
    lent = swap(lax.dynamic_index_in_dim(momentum, 1 - core, 1, keepdims=False))
    rows = shape((ROWS, FF), F32)
    packed_rows = len(BLOCKS) * LANE
    ns_input, new_mine, new_give, packed = call(
        momentum_kernel,
        [chunk, rows, rows, shape((packed_rows, LANE))],
        where,
        keep,
        go(up1, NEAR),
        go(up2, 2 * NEAR),
        go(down1, -NEAR),
        kept,
        lent,
        flops=2 * PAIR * FF * FF,
    )
    packed = packed.reshape(n_z, packed_rows // n_z, LANE)
    pieces = call(
        piece_kernel, shape(packed.shape, F32), lax.all_to_all(packed, "z", 0, 0), scalars=0
    )
    gram = lax.all_to_all(pieces, "z", 0, 0).reshape(packed_rows, LANE)

    new_other = swap(new_give)
    new_momentum = jnp.stack(
        [jnp.where(core == 0, new_mine, new_other), jnp.where(core == 0, new_other, new_mine)], axis=1
    )

    owner_ids = packing[:, 0]
    experts = owner_ids.shape[0]
    positions = jnp.arange(experts, dtype=jnp.int32)
    shared = (owner_ids[:, None] == owner_ids[None, :]) & (positions[None, :] < positions[:, None])
    target = owner_ids * MOST + jnp.sum(shared.astype(jnp.int32), axis=1)
    hits = target[None, :] == group * MOST + jnp.arange(MOST, dtype=jnp.int32)[:, None]
    lies = positions % CORES * n_owner + positions // CORES
    source = jnp.max(jnp.where(hits, lies[None, :], -1), axis=1)
    my_owner = lax.dynamic_slice_in_dim(owner_ids, group * CORES + core, 1, 0)

    sent = call(
        newton_schulz_kernel,
        shape((CORES, n_owner, ROWS, FF)),
        my_owner,
        gram,
        ns_input,
        flops=2 * 27 * FF * FF * FF,
    )
    got = lax.all_to_all(
        sent.reshape(CORES * n_owner, ROWS, FF), ("core", "expert"), 0, 0
    )
    stacked = call(
        stack_kernel,
        shape((ROWS, MOST, FF)),
        source,
        got,
        scratch=[pltpu.VMEM((ROWS, MOST, FF), F32)],
    )
    return new_momentum, stacked


def solution(mesh):
    n_dp, n_owner = mesh.devices.shape
    devices = np.asarray(mesh.devices).reshape(n_dp // CORES, CORES, n_owner)
    finer = Mesh(devices, ("z", "core", "expert"))
    spec = P(("z", "core"), "expert", None)
    return jax.shard_map(
        body, mesh=finer, in_specs=(spec,) * 4 + (P(),), out_specs=(spec, spec), check_vma=False
    )
```

```python
import functools
import math

import jax
import jax.numpy as jnp
import numpy as np
from jax import lax
from jax.experimental import pallas as pl
from jax.experimental.pallas import tpu as pltpu
from jax.sharding import Mesh
from jax.sharding import PartitionSpec as P

D = 2048
FF = 384
TILE = 256
ITERS = 3
MOST = 4
CORES = 2
NEAR = 4
FAR = 4
ROWS = 64
PAIR = CORES * ROWS
LANE = 128

COEF_A = 3.4445
COEF_B = -4.775
COEF_C = 2.0315
BETA = 0.95
EPSILON = 1e-07
BLOCKS = ((0, 0), (0, 1), (0, 2), (1, 1), (1, 2), (2, 2))
MIB = 1024 * 1024
VMEM = pl.BlockSpec(memory_space=pltpu.VMEM)
SMEM = pl.BlockSpec(memory_space=pltpu.SMEM)
BF16 = jnp.bfloat16
F32 = jnp.float32


def call(kernel, outs, *args, scalars=1, scratch=(), flops=0):
    many = isinstance(outs, list)
    nbytes = sum(a.size * a.dtype.itemsize for a in args)
    return pl.pallas_call(
        kernel,
        out_shape=outs,
        in_specs=[SMEM] * scalars + [VMEM] * (len(args) - scalars),
        out_specs=[VMEM] * len(outs) if many else VMEM,
        scratch_shapes=list(scratch),
        compiler_params=pltpu.CompilerParams(vmem_limit_bytes=16 * MIB),
        cost_estimate=pl.CostEstimate(flops=flops, bytes_accessed=nbytes, transcendentals=0),
    )(*args)


def shape(dims, dtype=BF16):
    return jax.ShapeDtypeStruct(dims, dtype)


def transposed_dot(x, y):
    return lax.dot_general(x, y, (((0,), (0,)), ((), ())), preferred_element_type=F32)


def partial_kernel(theirs, where_ref, acts_ref, grads_ref, out_ref, masked_ref):
    near_at, core = where_ref[0], where_ref[1]
    expert = 1 - core if theirs else core
    for tile in range(acts_ref.shape[0] // TILE):
        rows = slice(tile * TILE, (tile + 1) * TILE)
        factor = jnp.where(where_ref[2 + tile] == expert, 1.0, 0.0).astype(F32)
        masked_ref[rows, :] = (grads_ref[rows, :].astype(F32) * factor).astype(BF16)
    masked = masked_ref[...]
    for rel in range(NEAR):
        cls = lax.rem(near_at + rel, NEAR)
        for q in range(FAR):
            start = pl.multiple_of((q * NEAR + cls) * PAIR, PAIR)
            block = transposed_dot(acts_ref[:, pl.ds(start, PAIR)], masked)
            out_ref[rel, q] = block.astype(BF16)


def add_kernel(mine_ref, other_ref, own_ref, up1_ref, up2_ref, down2_ref, down1_ref):
    def total(rel, qs):
        return (mine_ref[rel, qs].astype(F32) + other_ref[rel, qs].astype(F32)).astype(BF16)

    half = FAR // 2
    own_ref[...] = total(0, slice(None))
    up1_ref[...] = total(1, slice(None))
    up2_ref[...] = total(2, slice(0, half))
    down2_ref[...] = total(2, slice(half, FAR))
    down1_ref[...] = total(3, slice(None))


def near_kernel(own_ref, a_ref, b_ref, c_ref, d_ref, out_ref):
    half = FAR // 2
    for q in range(FAR):
        last = c_ref[q] if q < half else d_ref[q - half]
        total = own_ref[q].astype(F32) + a_ref[q].astype(F32)
        out_ref[q] = (total + (b_ref[q].astype(F32) + last.astype(F32))).astype(BF16)


def momentum_kernel(
    where_ref, parts_ref, kept_ref, lent_ref, ns_ref, mine_ref, give_ref, gram_ref
):
    core = where_ref[1]
    for who, old_ref, new_ref in ((core, kept_ref, mine_ref), (1 - core, lent_ref, give_ref)):
        rows = pl.ds(pl.multiple_of(who * ROWS, ROWS), ROWS)
        grad = parts_ref[0, rows, :].astype(F32)
        for at in range(1, FAR):
            grad = grad + parts_ref[at, rows, :].astype(F32)
        new = BETA * old_ref[...] + grad
        new_ref[...] = new
        ns_ref[rows, :] = (grad + BETA * new).astype(BF16)
    x = ns_ref[...]
    gram = transposed_dot(x, x).astype(BF16)
    for at, (i, j) in enumerate(BLOCKS):
        gram_ref[at * LANE : (at + 1) * LANE, :] = gram[
            i * LANE : (i + 1) * LANE, j * LANE : (j + 1) * LANE
        ]


def spread_sum_kernel(parts_ref, out_ref):
    total = parts_ref[0].astype(F32)
    for at in range(1, parts_ref.shape[0]):
        total = total + parts_ref[at].astype(F32)
    for at in range(out_ref.shape[0]):
        out_ref[at] = total.astype(out_ref.dtype)


def split(x):
    high = x.astype(BF16)
    return high, (x - high.astype(F32)).astype(BF16)


def dot(x, y):
    return jnp.dot(x, y, preferred_element_type=F32)


def dot3(x, y):
    (xh, xl), (yh, yl) = x, y
    return dot(xh, yh) + (dot(xh, yl) + dot(xl, yh))


def newton_schulz_kernel(owner_ref, gram_ref, x_ref, out_ref):
    blocks = {}
    for at, (i, j) in enumerate(BLOCKS):
        block = gram_ref[at * LANE : (at + 1) * LANE, :]
        blocks[i, j] = block
        if i != j:
            blocks[j, i] = block.T
    gram = jnp.concatenate(
        [jnp.concatenate([blocks[i, j] for j in range(3)], axis=1) for i in range(3)], axis=0
    )
    rows = lax.broadcasted_iota(jnp.int32, (FF, FF), 0)
    cols = lax.broadcasted_iota(jnp.int32, (FF, FF), 1)
    eye = (rows == cols).astype(F32)
    trace = jnp.sum(jnp.sum(gram * eye, axis=1, keepdims=True), axis=0, keepdims=True)
    inv_norm = 1.0 / (jnp.sqrt(trace) + EPSILON)
    weights = gram * (inv_norm * inv_norm)
    current = x_ref[...].astype(F32) * inv_norm
    for sweep in range(ITERS):
        parts = split(weights)
        poly = COEF_A * eye + COEF_B * weights + COEF_C * dot3(parts, parts)
        poly_parts = split(poly)
        current = dot3(split(current), poly_parts)
        if sweep < ITERS - 1:
            weights = dot3(split(dot3(parts, poly_parts)), poly_parts)
    update = (current * math.sqrt(D)).astype(BF16)
    out_ref[...] = jnp.zeros_like(out_ref)
    for core in range(CORES):
        out_ref[core, owner_ref[0]] = update[core * ROWS : (core + 1) * ROWS, :]


def stack_kernel(source_ref, got_ref, out_ref, wide_ref):
    for slot in range(MOST):
        source = source_ref[slot]
        filled = jnp.where(source >= 0, 1.0, 0.0).astype(F32)
        wide_ref[:, slot, :] = got_ref[jnp.maximum(source, 0)].astype(F32) * filled
    out_ref[...] = wide_ref[...].astype(BF16)


def ring(size, step):
    return [(i, (i + step) % size) for i in range(size)]


def body(acts, grads, tile_expert, momentum, packing):
    near_at, core, group = (lax.axis_index(name) for name in ("near", "core", "expert"))
    n_owner = lax.axis_size("expert")
    where = jnp.concatenate([jnp.stack([near_at, core]), tile_expert[:, 0, 0]]).astype(jnp.int32)
    flat_acts, flat_grads = acts[:, 0, :], grads[:, 0, :]

    def go(value, step):
        return lax.ppermute(value, ("far", "near"), ring(FAR * NEAR, step))

    def swap(value):
        return lax.ppermute(value, "core", ring(CORES, 1))

    def partial_of(theirs):
        return call(
            functools.partial(partial_kernel, theirs),
            shape((NEAR, FAR, PAIR, FF)),
            where,
            flat_acts,
            flat_grads,
            scratch=[pltpu.VMEM(flat_grads.shape, BF16)],
            flops=2 * flat_acts.size * FF,
        )

    other = swap(partial_of(True))
    mine = partial_of(False)
    whole, half = shape((FAR, PAIR, FF)), shape((FAR // 2, PAIR, FF))
    own, up1, up2, down2, down1 = call(
        add_kernel, [whole, whole, half, half, whole], mine, other, scalars=0
    )
    chunk = shape((PAIR, FF))
    near = call(
        near_kernel,
        shape((FAR, PAIR, FF)),
        own,
        go(up1, 1),
        go(down1, -1),
        go(up2, 2),
        go(down2, -2),
        scalars=0,
    )
    kept = lax.dynamic_index_in_dim(momentum, core, 1, keepdims=False)
    lent = swap(lax.dynamic_index_in_dim(momentum, 1 - core, 1, keepdims=False))
    rows = shape((ROWS, FF), F32)
    packed_rows = len(BLOCKS) * LANE
    ns_input, new_mine, new_give, packed = call(
        momentum_kernel,
        [chunk, rows, rows, shape((packed_rows, LANE))],
        where,
        lax.all_to_all(near, "far", 0, 0),
        kept,
        lent,
        flops=2 * PAIR * FF * FF,
    )
    packed = packed.reshape(NEAR, packed_rows // NEAR, LANE)
    near_sum = call(spread_sum_kernel, shape(packed.shape), lax.all_to_all(packed, "near", 0, 0), scalars=0)
    far_sum = call(
        spread_sum_kernel,
        shape(packed.shape, F32),
        lax.all_to_all(near_sum, "far", 0, 0),
        scalars=0,
    )
    gram = lax.all_to_all(far_sum, "near", 0, 0).reshape(packed_rows, LANE)

    new_other = swap(new_give)
    new_momentum = jnp.stack(
        [jnp.where(core == 0, new_mine, new_other), jnp.where(core == 0, new_other, new_mine)], axis=1
    )

    owner_ids = packing[:, 0]
    experts = owner_ids.shape[0]
    positions = jnp.arange(experts, dtype=jnp.int32)
    shared = (owner_ids[:, None] == owner_ids[None, :]) & (positions[None, :] < positions[:, None])
    target = owner_ids * MOST + jnp.sum(shared.astype(jnp.int32), axis=1)
    hits = target[None, :] == group * MOST + jnp.arange(MOST, dtype=jnp.int32)[:, None]
    lies = positions % CORES * n_owner + positions // CORES
    source = jnp.max(jnp.where(hits, lies[None, :], -1), axis=1)
    my_owner = lax.dynamic_slice_in_dim(owner_ids, group * CORES + core, 1, 0)

    sent = call(
        newton_schulz_kernel,
        shape((CORES, n_owner, ROWS, FF)),
        my_owner,
        gram,
        ns_input,
        flops=2 * 27 * FF * FF * FF,
    )
    got = lax.all_to_all(
        sent.reshape(CORES * n_owner, ROWS, FF), ("core", "expert"), 0, 0
    )
    stacked = call(
        stack_kernel,
        shape((ROWS, MOST, FF)),
        source,
        got,
        scratch=[pltpu.VMEM((ROWS, MOST, FF), F32)],
    )
    return new_momentum, stacked


def solution(mesh):
    n_owner = mesh.devices.shape[1]
    devices = np.asarray(mesh.devices).reshape(FAR, NEAR, CORES, n_owner)
    finer = Mesh(devices, ("far", "near", "core", "expert"))
    spec = P(("far", "near", "core"), "expert", None)
    return jax.shard_map(
        body, mesh=finer, in_specs=(spec,) * 4 + (P(),), out_specs=(spec, spec), check_vma=False
    )
```

```python
import functools
import math

import jax
import jax.numpy as jnp
import numpy as np
from jax import lax
from jax.experimental import pallas as pl
from jax.experimental.pallas import tpu as pltpu
from jax.sharding import Mesh
from jax.sharding import PartitionSpec as P

D = 2048
FF = 384
TILE = 256
ITERS = 3
MOST = 4
CORES = 2
NEAR = 4
FAR = 4
ROWS = 64
PAIR = CORES * ROWS
LANE = 128

COEF_A = 3.4445
COEF_B = -4.775
COEF_C = 2.0315
BETA = 0.95
EPSILON = 1e-07
BLOCKS = ((0, 0), (0, 1), (0, 2), (1, 1), (1, 2), (2, 2))
MIB = 1024 * 1024
VMEM = pl.BlockSpec(memory_space=pltpu.VMEM)
SMEM = pl.BlockSpec(memory_space=pltpu.SMEM)
BF16 = jnp.bfloat16
F32 = jnp.float32


def call(kernel, args, outs, scalars=0, scratch=(), flops=0):
    many = isinstance(outs, list)
    nbytes = sum(a.size * a.dtype.itemsize for a in args)
    return pl.pallas_call(
        kernel,
        out_shape=outs,
        in_specs=[SMEM] * scalars + [VMEM] * (len(args) - scalars),
        out_specs=[VMEM] * len(outs) if many else VMEM,
        scratch_shapes=list(scratch),
        compiler_params=pltpu.CompilerParams(vmem_limit_bytes=16 * MIB),
        cost_estimate=pl.CostEstimate(flops=flops, bytes_accessed=nbytes, transcendentals=0),
    )(*args)


def shape(dims, dtype=BF16):
    return jax.ShapeDtypeStruct(dims, dtype)


def transposed_dot(x, y):
    return lax.dot_general(x, y, (((0,), (0,)), ((), ())), preferred_element_type=F32)


def masked_grads(expert, ids_ref, grads_ref, masked_ref):
    for tile in range(grads_ref.shape[0] // TILE):
        rows = slice(tile * TILE, (tile + 1) * TILE)
        factor = jnp.where(ids_ref[tile] == expert, 1.0, 0.0).astype(F32)
        masked_ref[rows, :] = (grads_ref[rows, :].astype(F32) * factor).astype(BF16)
    return masked_ref[...]


def chunk_rows(q, rel):
    at = lax.rem(lax.axis_index("near") + rel, NEAR)
    return pl.ds(pl.multiple_of((q * NEAR + at) * PAIR, PAIR), PAIR)


def partial_kernel(theirs, ids_ref, acts_ref, grads_ref, out_ref, masked_ref):
    core = lax.axis_index("core")
    masked = masked_grads(1 - core if theirs else core, ids_ref, grads_ref, masked_ref)
    for rel in range(NEAR):
        for q in range(FAR):
            block = transposed_dot(acts_ref[:, chunk_rows(q, rel)], masked)
            out_ref[rel, q] = block.astype(BF16)


def add_kernel(mine_ref, other_ref, own_ref, up1_ref, up2_ref, down2_ref, down1_ref):
    def total(rel, qs):
        return (mine_ref[rel, qs].astype(F32) + other_ref[rel, qs].astype(F32)).astype(BF16)

    half = FAR // 2
    own_ref[...] = total(0, slice(None))
    up1_ref[...] = total(1, slice(None))
    up2_ref[...] = total(2, slice(0, half))
    down2_ref[...] = total(2, slice(half, FAR))
    down1_ref[...] = total(3, slice(None))


def near_kernel(own_ref, c_ref, d_ref, a_ref, b_ref, out_ref):
    half = FAR // 2
    for q in range(FAR):
        last = c_ref[q] if q < half else d_ref[q - half]
        total = own_ref[q].astype(F32) + a_ref[q].astype(F32)
        out_ref[q] = (total + (b_ref[q].astype(F32) + last.astype(F32))).astype(BF16)


def momentum_kernel(
    parts_ref, kept_ref, lent_ref, ns_ref, mine_ref, give_ref, gram_ref
):
    core = lax.axis_index("core")
    for who, old_ref, new_ref in ((core, kept_ref, mine_ref), (1 - core, lent_ref, give_ref)):
        rows = pl.ds(pl.multiple_of(who * ROWS, ROWS), ROWS)
        grad = parts_ref[0, rows, :].astype(F32)
        for at in range(1, FAR):
            grad = grad + parts_ref[at, rows, :].astype(F32)
        new = BETA * old_ref[...] + grad
        new_ref[...] = new
        ns_ref[rows, :] = (grad + BETA * new).astype(BF16)
    x = ns_ref[...]
    gram = transposed_dot(x, x).astype(BF16)
    for at, (i, j) in enumerate(BLOCKS):
        gram_ref[at * LANE : (at + 1) * LANE, :] = gram[
            i * LANE : (i + 1) * LANE, j * LANE : (j + 1) * LANE
        ]


def spread_sum_kernel(parts_ref, out_ref):
    total = parts_ref[0].astype(F32)
    for at in range(1, parts_ref.shape[0]):
        total = total + parts_ref[at].astype(F32)
    for at in range(out_ref.shape[0]):
        out_ref[at] = total.astype(out_ref.dtype)


def split(x):
    high = x.astype(BF16)
    return high, (x - high.astype(F32)).astype(BF16)


def dot(x, y):
    return jnp.dot(x, y, preferred_element_type=F32)


def dot3(x, y):
    (xh, xl), (yh, yl) = x, y
    return dot(jnp.concatenate([xh, xl, xh], axis=1), jnp.concatenate([yh, yh, yl], axis=0))


def newton_schulz_kernel(owner_ref, gram_ref, x_ref, out_ref):
    blocks = {}
    for at, (i, j) in enumerate(BLOCKS):
        block = gram_ref[at * LANE : (at + 1) * LANE, :]
        blocks[i, j] = block
        if i != j:
            blocks[j, i] = block.T
    gram = jnp.concatenate(
        [jnp.concatenate([blocks[i, j] for j in range(3)], axis=1) for i in range(3)], axis=0
    )
    rows = lax.broadcasted_iota(jnp.int32, (FF, FF), 0)
    cols = lax.broadcasted_iota(jnp.int32, (FF, FF), 1)
    eye = (rows == cols).astype(F32)
    trace = jnp.sum(jnp.sum(gram * eye, axis=1, keepdims=True), axis=0, keepdims=True)
    inv_norm = 1.0 / (jnp.sqrt(trace) + EPSILON)
    weights = gram * (inv_norm * inv_norm)
    current = x_ref[...].astype(F32) * inv_norm
    for sweep in range(ITERS):
        parts = split(weights)
        poly = COEF_A * eye + COEF_B * weights + COEF_C * dot3(parts, parts)
        poly_parts = split(poly)
        current = dot3(split(current), poly_parts)
        if sweep < ITERS - 1:
            weights = dot3(split(dot3(parts, poly_parts)), poly_parts)
    update = (current * math.sqrt(D)).astype(BF16)
    out_ref[...] = jnp.zeros_like(out_ref)
    for core in range(CORES):
        out_ref[core, lax.rem(owner_ref[0], out_ref.shape[1])] = update[core * ROWS : (core + 1) * ROWS, :]


def place_kernel(source_ref, got_ref, out_ref):
    out_ref[...] = jnp.zeros_like(out_ref)
    for owner in range(out_ref.shape[0]):
        for slot in range(MOST):
            source = source_ref[owner * MOST + slot]

            @pl.when(source >= 0)
            def _():
                out_ref[owner, slot] = got_ref[source]


def stack_kernel(source_ref, got_ref, out_ref, wide_ref):
    for slot in range(MOST):
        source = source_ref[slot]
        filled = jnp.where(source >= 0, 1.0, 0.0).astype(F32)
        wide_ref[:, slot, :] = got_ref[jnp.maximum(source, 0), slot].astype(F32) * filled
    out_ref[...] = wide_ref[...].astype(BF16)


def ring(size, step):
    return [(i, (i + step) % size) for i in range(size)]


def body(acts, grads, tile_expert, momentum, packing):
    core, x, y = (lax.axis_index(name) for name in ("core", "x", "y"))
    n_x, n_y = lax.axis_size("x"), lax.axis_size("y")
    flat_acts, flat_grads = acts[:, 0, :], grads[:, 0, :]

    def go(value, step):
        return lax.ppermute(value, ("far", "near"), ring(FAR * NEAR, step))

    def swap(value):
        return lax.ppermute(value, "core", ring(CORES, 1))

    def partial_of(theirs):
        return call(
            functools.partial(partial_kernel, theirs),
            (tile_expert[:, 0, 0], flat_acts, flat_grads),
            shape((NEAR, FAR, PAIR, FF)),
            scalars=1,
            scratch=[pltpu.VMEM(flat_grads.shape, BF16)],
            flops=2 * flat_acts.size * FF,
        )

    other = swap(partial_of(True))
    mine = partial_of(False)
    whole, half = shape((FAR, PAIR, FF)), shape((FAR // 2, PAIR, FF))
    own, up1, up2, down2, down1 = call(
        add_kernel, (mine, other), [whole, whole, half, half, whole]
    )
    chunk = shape((PAIR, FF))
    arrived = (go(up2, 2), go(down2, -2), go(up1, 1), go(down1, -1))
    near = call(near_kernel, (own, *arrived), shape((FAR, PAIR, FF)))
    kept = lax.dynamic_index_in_dim(momentum, core, 1, keepdims=False)
    lent = swap(lax.dynamic_index_in_dim(momentum, 1 - core, 1, keepdims=False))
    rows = shape((ROWS, FF), F32)
    packed_rows = len(BLOCKS) * LANE
    ns_input, new_mine, new_give, packed = call(
        momentum_kernel,
        (lax.all_to_all(near, "far", 0, 0), kept, lent),
        [chunk, rows, rows, shape((packed_rows, LANE))],
        flops=2 * PAIR * FF * FF,
    )
    packed = packed.reshape(NEAR, packed_rows // NEAR, LANE)
    near_parts = lax.all_to_all(packed, "near", 0, 0)
    near_sum = call(spread_sum_kernel, (near_parts,), shape(packed.shape))
    far_parts = lax.all_to_all(near_sum, "far", 0, 0)
    far_sum = call(spread_sum_kernel, (far_parts,), shape(packed.shape, F32))
    gram = lax.all_to_all(far_sum, "near", 0, 0).reshape(packed_rows, LANE)

    new_other = swap(new_give)
    new_momentum = jnp.stack(
        [jnp.where(core == 0, new_mine, new_other), jnp.where(core == 0, new_other, new_mine)], axis=1
    )

    owner_ids = packing[:, 0]
    experts = owner_ids.shape[0]
    positions = jnp.arange(experts, dtype=jnp.int32)
    shared = (owner_ids[:, None] == owner_ids[None, :]) & (positions[None, :] < positions[:, None])
    target = owner_ids * MOST + jnp.sum(shared.astype(jnp.int32), axis=1)
    of_core, of_y = positions % CORES, positions // CORES % n_y
    of_x = positions // (CORES * n_y)
    slots = jnp.arange(MOST, dtype=jnp.int32)
    line = (jnp.arange(n_x, dtype=jnp.int32)[:, None] * n_y + y) * MOST + slots[None, :]
    passes = (line.reshape(-1)[:, None] == target[None, :]) & (of_x == x)[None, :]
    placed_from = jnp.max(jnp.where(passes, (of_core * n_y + of_y)[None, :], -1), axis=1)
    fills = ((x * n_y + y) * MOST + slots)[:, None] == target[None, :]
    stacked_from = jnp.max(jnp.where(fills, of_x[None, :], -1), axis=1)
    my_owner = lax.dynamic_slice_in_dim(owner_ids, (x * n_y + y) * CORES + core, 1, 0)

    sent = call(
        newton_schulz_kernel,
        (my_owner, gram, ns_input),
        shape((CORES, n_y, ROWS, FF)),
        scalars=1,
        flops=2 * 27 * FF * FF * FF,
    )
    got = lax.all_to_all(sent.reshape(CORES * n_y, ROWS, FF), ("core", "y"), 0, 0)
    placed = call(place_kernel, (placed_from, got), shape((n_x, MOST, ROWS, FF)), scalars=1)
    got = lax.all_to_all(placed, "x", 0, 0)
    stacked = call(
        stack_kernel,
        (stacked_from, got),
        shape((ROWS, MOST, FF)),
        scalars=1,
        scratch=[pltpu.VMEM((ROWS, MOST, FF), F32)],
    )
    return new_momentum, stacked


def solution(mesh):
    devices = np.asarray(mesh.devices)
    side = math.isqrt(devices.shape[1])
    devices = devices.reshape(FAR, NEAR, CORES, side, side)
    finer = Mesh(devices, ("far", "near", "core", "x", "y"))
    spec = P(("far", "near", "core"), ("x", "y"), None)
    return jax.shard_map(
        body, mesh=finer, in_specs=(spec,) * 4 + (P(),), out_specs=(spec, spec), check_vma=False
    )
```

```python
import functools
import math

import jax
import jax.numpy as jnp
import numpy as np
from jax import lax
from jax.experimental import pallas as pl
from jax.experimental.pallas import tpu as pltpu
from jax.sharding import Mesh
from jax.sharding import PartitionSpec as P

D = 2048
FF = 384
TILE = 256
ITERS = 3
MOST = 4
CORES = 2
NEAR = 4
FAR = 4
ROWS = 64
PAIR = CORES * ROWS
LANE = 128

COEF_A = 3.4445
COEF_B = -4.775
COEF_C = 2.0315
BETA = 0.95
EPSILON = 1e-07
BLOCKS = ((0, 0), (0, 1), (0, 2), (1, 1), (1, 2), (2, 2))
MIB = 1024 * 1024
VMEM = pl.BlockSpec(memory_space=pltpu.VMEM)
ANY = pl.BlockSpec(memory_space=pl.ANY)
SMEM = pl.BlockSpec(memory_space=pltpu.SMEM)
BF16 = jnp.bfloat16
F32 = jnp.float32


def call(kernel, args, outs, scalars=0, scratch=(), flops=0, spaces=None):
    many = isinstance(outs, list)
    nbytes = sum(a.size * a.dtype.itemsize for a in args)
    return pl.pallas_call(
        kernel,
        out_shape=outs,
        in_specs=[SMEM] * scalars + [VMEM] * (len(args) - scalars),
        out_specs=spaces or ([VMEM] * len(outs) if many else VMEM),
        scratch_shapes=list(scratch),
        compiler_params=pltpu.CompilerParams(vmem_limit_bytes=16 * MIB),
        cost_estimate=pl.CostEstimate(flops=flops, bytes_accessed=nbytes, transcendentals=0),
    )(*args)


def shape(dims, dtype=BF16):
    return jax.ShapeDtypeStruct(dims, dtype)


def transposed_dot(x, y):
    return lax.dot_general(x, y, (((0,), (0,)), ((), ())), preferred_element_type=F32)


def masked_grads(expert, ids_ref, grads_ref, masked_ref):
    for tile in range(grads_ref.shape[0] // TILE):
        rows = slice(tile * TILE, (tile + 1) * TILE)
        factor = jnp.where(ids_ref[tile] == expert, 1.0, 0.0).astype(F32)
        masked_ref[rows, :] = (grads_ref[rows, :].astype(F32) * factor).astype(BF16)
    return masked_ref[...]


def chunk_rows(q, rel):
    at = lax.rem(lax.axis_index("near") + rel, NEAR)
    return pl.ds(pl.multiple_of((q * NEAR + at) * PAIR, PAIR), PAIR)


def partial_kernel(theirs, ids_ref, acts_ref, grads_ref, out_ref, masked_ref):
    core = lax.axis_index("core")
    masked = masked_grads(1 - core if theirs else core, ids_ref, grads_ref, masked_ref)
    for rel in range(NEAR):
        for q in range(FAR):
            block = transposed_dot(acts_ref[:, chunk_rows(q, rel)], masked)
            out_ref[rel, q] = block.astype(BF16)


def add_kernel(mine_ref, other_ref, own_ref, up1_ref, up2_ref, down2_ref, down1_ref):
    def total(rel, qs):
        return (mine_ref[rel, qs].astype(F32) + other_ref[rel, qs].astype(F32)).astype(BF16)

    half = FAR // 2
    own_ref[...] = total(0, slice(None))
    up1_ref[...] = total(1, slice(None))
    up2_ref[...] = total(2, slice(0, half))
    down2_ref[...] = total(2, slice(half, FAR))
    down1_ref[...] = total(3, slice(None))


def near_kernel(own_ref, c_ref, d_ref, a_ref, b_ref, out_ref):
    half = FAR // 2
    for q in range(FAR):
        last = c_ref[q] if q < half else d_ref[q - half]
        total = own_ref[q].astype(F32) + a_ref[q].astype(F32)
        out_ref[q] = (total + (b_ref[q].astype(F32) + last.astype(F32))).astype(BF16)


def momentum_kernel(
    parts_ref, kept_ref, lent_ref, ns_ref, mine_ref, give_ref, gram_ref
):
    core = lax.axis_index("core")
    for who, old_ref, new_ref in ((core, kept_ref, mine_ref), (1 - core, lent_ref, give_ref)):
        rows = pl.ds(pl.multiple_of(who * ROWS, ROWS), ROWS)
        grad = parts_ref[0, rows, :].astype(F32)
        for at in range(1, FAR):
            grad = grad + parts_ref[at, rows, :].astype(F32)
        new = BETA * old_ref[...] + grad
        new_ref[...] = new
        ns_ref[rows, :] = (grad + BETA * new).astype(BF16)
    x = ns_ref[...]
    gram = transposed_dot(x, x).astype(BF16)
    for at, (i, j) in enumerate(BLOCKS):
        gram_ref[at * LANE : (at + 1) * LANE, :] = gram[
            i * LANE : (i + 1) * LANE, j * LANE : (j + 1) * LANE
        ]


def spread_sum_kernel(parts_ref, out_ref):
    total = parts_ref[0].astype(F32)
    for at in range(1, parts_ref.shape[0]):
        total = total + parts_ref[at].astype(F32)
    for at in range(out_ref.shape[0]):
        out_ref[at] = total.astype(out_ref.dtype)


def split(x):
    high = x.astype(BF16)
    return high, (x - high.astype(F32)).astype(BF16)


def dot(x, y):
    return jnp.dot(x, y, preferred_element_type=F32)


def dot3(x, y):
    (xh, xl), (yh, yl) = x, y
    return dot(jnp.concatenate([xh, xl, xh], axis=1), jnp.concatenate([yh, yh, yl], axis=0))


def newton_schulz_kernel(
    owner_ref, gram_ref, x_ref, mine_ref, other_ref, out_ref, new_ref, update_ref, sems
):
    first = lax.axis_index("core") == 0
    new_ref[:, 0, :] = jnp.where(first, mine_ref[...], other_ref[...])
    new_ref[:, 1, :] = jnp.where(first, other_ref[...], mine_ref[...])
    blocks = {}
    for at, (i, j) in enumerate(BLOCKS):
        block = gram_ref[at * LANE : (at + 1) * LANE, :]
        blocks[i, j] = block
        if i != j:
            blocks[j, i] = block.T
    gram = jnp.concatenate(
        [jnp.concatenate([blocks[i, j] for j in range(3)], axis=1) for i in range(3)], axis=0
    )
    rows = lax.broadcasted_iota(jnp.int32, (FF, FF), 0)
    cols = lax.broadcasted_iota(jnp.int32, (FF, FF), 1)
    eye = (rows == cols).astype(F32)
    trace = jnp.sum(jnp.sum(gram * eye, axis=1, keepdims=True), axis=0, keepdims=True)
    inv_norm = 1.0 / (jnp.sqrt(trace) + EPSILON)
    weights = gram * (inv_norm * inv_norm)
    current = x_ref[...].astype(F32) * inv_norm
    for sweep in range(ITERS):
        parts = split(weights)
        poly = COEF_A * eye + COEF_B * weights + COEF_C * dot3(parts, parts)
        poly_parts = split(poly)
        current = dot3(split(current), poly_parts)
        if sweep < ITERS - 1:
            weights = dot3(split(dot3(parts, poly_parts)), poly_parts)
    update_ref[...] = (current * math.sqrt(D)).astype(BF16)
    copies = [
        pltpu.make_async_copy(
            update_ref.at[pl.ds(core * ROWS, ROWS), :], out_ref.at[core, owner_ref[0]], sems.at[core]
        )
        for core in range(CORES)
    ]
    for copy in copies:
        copy.start()
    for copy in copies:
        copy.wait()


def stack_kernel(source_ref, got_ref, out_ref, wide_ref):
    for slot in range(MOST):
        source = source_ref[slot]
        taken = got_ref[jnp.maximum(source, 0)].astype(F32)
        wide_ref[:, slot, :] = jnp.where(source >= 0, taken, jnp.zeros_like(taken))
    out_ref[...] = wide_ref[...].astype(BF16)


def ring(size, step):
    return [(i, (i + step) % size) for i in range(size)]


def body(acts, grads, tile_expert, momentum, packing):
    core, x, y = (lax.axis_index(name) for name in ("core", "x", "y"))
    n_x, n_y = lax.axis_size("x"), lax.axis_size("y")
    flat_acts, flat_grads = acts[:, 0, :], grads[:, 0, :]

    def go(value, step):
        return lax.ppermute(value, ("far", "near"), ring(FAR * NEAR, step))

    def swap(value):
        return lax.ppermute(value, "core", ring(CORES, 1))

    def partial_of(theirs):
        return call(
            functools.partial(partial_kernel, theirs),
            (tile_expert[:, 0, 0], flat_acts, flat_grads),
            shape((NEAR, FAR, PAIR, FF)),
            scalars=1,
            scratch=[pltpu.VMEM(flat_grads.shape, BF16)],
            flops=2 * flat_acts.size * FF,
        )

    other = swap(partial_of(True))
    mine = partial_of(False)
    whole, half = shape((FAR, PAIR, FF)), shape((FAR // 2, PAIR, FF))
    own, up1, up2, down2, down1 = call(
        add_kernel, (mine, other), [whole, whole, half, half, whole]
    )
    chunk = shape((PAIR, FF))
    arrived = (go(up2, 2), go(down2, -2), go(up1, 1), go(down1, -1))
    near = call(near_kernel, (own, *arrived), shape((FAR, PAIR, FF)))
    kept = lax.dynamic_index_in_dim(momentum, core, 1, keepdims=False)
    lent = swap(lax.dynamic_index_in_dim(momentum, 1 - core, 1, keepdims=False))
    rows = shape((ROWS, FF), F32)
    packed_rows = len(BLOCKS) * LANE
    ns_input, new_mine, new_give, packed = call(
        momentum_kernel,
        (lax.all_to_all(near, "far", 0, 0), kept, lent),
        [chunk, rows, rows, shape((packed_rows, LANE))],
        flops=2 * PAIR * FF * FF,
    )
    packed = packed.reshape(NEAR, packed_rows // NEAR, LANE)
    near_parts = lax.all_to_all(packed, "near", 0, 0)
    near_sum = call(spread_sum_kernel, (near_parts,), shape(packed.shape))
    far_parts = lax.all_to_all(near_sum, "far", 0, 0)
    far_sum = call(spread_sum_kernel, (far_parts,), shape(packed.shape, F32))
    gram = lax.all_to_all(far_sum, "near", 0, 0).reshape(packed_rows, LANE)

    new_other = swap(new_give)
    owner_ids = packing[:, 0]
    experts = owner_ids.shape[0]
    positions = jnp.arange(experts, dtype=jnp.int32)
    shared = (owner_ids[:, None] == owner_ids[None, :]) & (positions[None, :] < positions[:, None])
    target = owner_ids * MOST + jnp.sum(shared.astype(jnp.int32), axis=1)
    n_owner = n_x * n_y
    lies = positions % CORES * n_owner + positions // CORES
    wanted = (x * n_y + y) * MOST + jnp.arange(MOST, dtype=jnp.int32)
    fills = wanted[:, None] == target[None, :]
    stacked_from = jnp.max(jnp.where(fills, lies[None, :], -1), axis=1)
    my_owner = lax.dynamic_slice_in_dim(owner_ids, (x * n_y + y) * CORES + core, 1, 0)

    sent, new_momentum = call(
        newton_schulz_kernel,
        (my_owner, gram, ns_input, new_mine, new_other),
        [shape((CORES, n_owner, ROWS, FF)), shape((ROWS, CORES, FF), F32)],
        scalars=1,
        scratch=[pltpu.VMEM((PAIR, FF), BF16), pltpu.SemaphoreType.DMA((CORES,))],
        flops=2 * 27 * FF * FF * FF,
        spaces=[ANY, VMEM],
    )
    got = lax.all_to_all(sent.reshape(CORES * n_owner, ROWS, FF), ("core", "x", "y"), 0, 0)
    stacked = call(
        stack_kernel,
        (stacked_from, got),
        shape((ROWS, MOST, FF)),
        scalars=1,
        scratch=[pltpu.VMEM((ROWS, MOST, FF), F32)],
    )
    return new_momentum, stacked


def solution(mesh):
    devices = np.asarray(mesh.devices)
    side = math.isqrt(devices.shape[1])
    devices = devices.reshape(FAR, NEAR, CORES, side, side)
    finer = Mesh(devices, ("far", "near", "core", "x", "y"))
    spec = P(("far", "near", "core"), ("x", "y"), None)
    return jax.shard_map(
        body, mesh=finer, in_specs=(spec,) * 4 + (P(),), out_specs=(spec, spec), check_vma=False
    )
```

```python
import functools
import math

import jax
import jax.numpy as jnp
import numpy as np
from jax import lax
from jax.experimental import pallas as pl
from jax.experimental.pallas import tpu as pltpu
from jax.sharding import Mesh
from jax.sharding import PartitionSpec as P

D = 2048
FF = 384
TILE = 256
ITERS = 3
MOST = 4
CORES = 2
NEAR = 4
FAR = 4
ROWS = 64
PAIR = CORES * ROWS
LANE = 128

COEF_A = 3.4445
COEF_B = -4.775
COEF_C = 2.0315
BETA = 0.95
EPSILON = 1e-07
BLOCKS = ((0, 1), (0, 2), (1, 2))
SIDE = FF // LANE
HALF = LANE // 2
PACKED = len(BLOCKS) * LANE + (SIDE + 2) * HALF
MIB = 1024 * 1024
VMEM = pl.BlockSpec(memory_space=pltpu.VMEM)
SMEM = pl.BlockSpec(memory_space=pltpu.SMEM)
BF16 = jnp.bfloat16
F32 = jnp.float32


def call(kernel, args, outs, scalars=0, scratch=(), flops=0):
    many = isinstance(outs, list)
    nbytes = sum(a.size * a.dtype.itemsize for a in args)
    return pl.pallas_call(
        kernel,
        out_shape=outs,
        in_specs=[SMEM] * scalars + [VMEM] * (len(args) - scalars),
        out_specs=[VMEM] * len(outs) if many else VMEM,
        scratch_shapes=list(scratch),
        compiler_params=pltpu.CompilerParams(vmem_limit_bytes=16 * MIB),
        cost_estimate=pl.CostEstimate(flops=flops, bytes_accessed=nbytes, transcendentals=0),
    )(*args)


def shape(dims, dtype=BF16):
    return jax.ShapeDtypeStruct(dims, dtype)


def transposed_dot(x, y):
    return lax.dot_general(x, y, (((0,), (0,)), ((), ())), preferred_element_type=F32)


def masked_grads(expert, ids_ref, grads_ref, masked_ref):
    for tile in range(grads_ref.shape[0] // TILE):
        rows = slice(tile * TILE, (tile + 1) * TILE)
        factor = jnp.where(ids_ref[tile] == expert, 1.0, 0.0).astype(F32)
        masked_ref[rows, :] = (grads_ref[rows, :].astype(F32) * factor).astype(BF16)
    return masked_ref[...]


def chunk_rows(q, rel):
    at = lax.rem(lax.axis_index("near") + rel, NEAR)
    return pl.ds(pl.multiple_of((q * NEAR + at) * PAIR, PAIR), PAIR)


def partial_kernel(theirs, ids_ref, acts_ref, grads_ref, out_ref, masked_ref):
    core = lax.axis_index("core")
    masked = masked_grads(1 - core if theirs else core, ids_ref, grads_ref, masked_ref)
    for rel in range(NEAR):
        for q in range(FAR):
            block = transposed_dot(acts_ref[:, chunk_rows(q, rel)], masked)
            out_ref[rel, q] = block.astype(BF16)


def add_kernel(mine_ref, other_ref, own_ref, up1_ref, up2_ref, down2_ref, down1_ref):
    def total(rel, qs):
        return (mine_ref[rel, qs].astype(F32) + other_ref[rel, qs].astype(F32)).astype(BF16)

    half = FAR // 2
    own_ref[...] = total(0, slice(None))
    up1_ref[...] = total(1, slice(None))
    up2_ref[...] = total(2, slice(0, half))
    down2_ref[...] = total(2, slice(half, FAR))
    down1_ref[...] = total(3, slice(None))


def near_kernel(own_ref, c_ref, d_ref, a_ref, b_ref, out_ref):
    half = FAR // 2
    for q in range(FAR):
        last = c_ref[q] if q < half else d_ref[q - half]
        total = own_ref[q].astype(F32) + a_ref[q].astype(F32)
        out_ref[q] = (total + (b_ref[q].astype(F32) + last.astype(F32))).astype(BF16)


def momentum_kernel(
    parts_ref, kept_ref, lent_ref, ns_ref, mine_ref, give_ref, gram_ref
):
    core = lax.axis_index("core")
    for who, old_ref, new_ref in ((core, kept_ref, mine_ref), (1 - core, lent_ref, give_ref)):
        rows = pl.ds(pl.multiple_of(who * ROWS, ROWS), ROWS)
        grad = parts_ref[0, rows, :].astype(F32)
        for at in range(1, FAR):
            grad = grad + parts_ref[at, rows, :].astype(F32)
        new = BETA * old_ref[...] + grad
        new_ref[...] = new
        ns_ref[rows, :] = (grad + BETA * new).astype(BF16)
    x = ns_ref[...]
    gram = transposed_dot(x, x)
    top, bottom = [], []
    for i in range(SIDE):
        columns = slice(i * LANE, (i + 1) * LANE)
        top.append(gram[i * LANE : i * LANE + HALF, columns])
        bottom.append(gram[i * LANE + HALF : (i + 1) * LANE, columns])
    left = lax.broadcasted_iota(jnp.int32, (HALF, LANE), 1) < HALF
    pair = jnp.where(left, pltpu.roll(bottom[0], HALF, 1), bottom[1])
    whole = [gram[i * LANE : (i + 1) * LANE, j * LANE : (j + 1) * LANE] for i, j in BLOCKS]
    at = 0
    for part in whole + top + [pair, bottom[2]]:
        gram_ref[at : at + part.shape[0], :] = part.astype(BF16)
        at += part.shape[0]


def spread_sum_kernel(parts_ref, out_ref):
    total = parts_ref[0].astype(F32)
    for at in range(1, parts_ref.shape[0]):
        total = total + parts_ref[at].astype(F32)
    for at in range(out_ref.shape[0]):
        out_ref[at] = total.astype(out_ref.dtype)


def split(x):
    high = x.astype(BF16)
    return high, (x - high.astype(F32)).astype(BF16)


def dot(x, y):
    return jnp.dot(x, y, preferred_element_type=F32)


def dot3(x, y):
    (xh, xl), (yh, yl) = x, y
    return dot(jnp.concatenate([xh, xl, xh], axis=1), jnp.concatenate([yh, yh, yl], axis=0))


def newton_schulz_kernel(owner_ref, gram_ref, x_ref, out_ref):
    blocks = {}
    for at, (i, j) in enumerate(BLOCKS):
        block = gram_ref[at * LANE : (at + 1) * LANE, :]
        blocks[i, j], blocks[j, i] = block, block.T
    start = len(BLOCKS) * LANE
    halves = [gram_ref[start + i * HALF : start + (i + 1) * HALF, :] for i in range(SIDE + 2)]
    left = lax.broadcasted_iota(jnp.int32, (HALF, LANE), 1) < HALF
    corners = (pltpu.roll(halves[SIDE], HALF, 1), halves[SIDE], halves[SIDE + 1])
    for i in range(SIDE):
        turned = jnp.concatenate([halves[i], halves[i]], axis=0).T
        below = jnp.where(left, turned[HALF:, :], corners[i])
        blocks[i, i] = jnp.concatenate([halves[i], below], axis=0)
    gram = jnp.concatenate(
        [jnp.concatenate([blocks[i, j] for j in range(3)], axis=1) for i in range(3)], axis=0
    )
    rows = lax.broadcasted_iota(jnp.int32, (FF, FF), 0)
    cols = lax.broadcasted_iota(jnp.int32, (FF, FF), 1)
    eye = (rows == cols).astype(F32)
    trace = jnp.sum(jnp.sum(gram * eye, axis=1, keepdims=True), axis=0, keepdims=True)
    inv_norm = 1.0 / (jnp.sqrt(trace) + EPSILON)
    weights = gram * (inv_norm * inv_norm)
    current = x_ref[...].astype(F32) * inv_norm
    for sweep in range(ITERS):
        parts = split(weights)
        poly = COEF_A * eye + COEF_B * weights + COEF_C * dot3(parts, parts)
        poly_parts = split(poly)
        current = dot3(split(current), poly_parts)
        if sweep < ITERS - 1:
            weights = dot3(split(dot3(parts, poly_parts)), poly_parts)
    update = (current * math.sqrt(D)).astype(BF16)
    out_ref[...] = jnp.zeros_like(out_ref)
    for core in range(CORES):
        out_ref[core, lax.rem(owner_ref[0], out_ref.shape[1])] = update[core * ROWS : (core + 1) * ROWS, :]


def place_kernel(source_ref, got_ref, out_ref):
    out_ref[...] = jnp.zeros_like(out_ref)
    for owner in range(out_ref.shape[0]):
        for slot in range(MOST):
            source = source_ref[owner * MOST + slot]

            @pl.when(source >= 0)
            def _():
                out_ref[owner, slot] = got_ref[source]


def stack_kernel(source_ref, got_ref, out_ref, wide_ref):
    for slot in range(MOST):
        source = source_ref[slot]
        filled = jnp.where(source >= 0, 1.0, 0.0).astype(F32)
        wide_ref[:, slot, :] = got_ref[jnp.maximum(source, 0), slot].astype(F32) * filled
    out_ref[...] = wide_ref[...].astype(BF16)


def ring(size, step):
    return [(i, (i + step) % size) for i in range(size)]


def body(acts, grads, tile_expert, momentum, packing):
    core, x, y = (lax.axis_index(name) for name in ("core", "x", "y"))
    n_x, n_y = lax.axis_size("x"), lax.axis_size("y")
    flat_acts, flat_grads = acts[:, 0, :], grads[:, 0, :]

    def go(value, step):
        return lax.ppermute(value, ("far", "near"), ring(FAR * NEAR, step))

    def swap(value):
        return lax.ppermute(value, "core", ring(CORES, 1))

    def partial_of(theirs):
        return call(
            functools.partial(partial_kernel, theirs),
            (tile_expert[:, 0, 0], flat_acts, flat_grads),
            shape((NEAR, FAR, PAIR, FF)),
            scalars=1,
            scratch=[pltpu.VMEM(flat_grads.shape, BF16)],
            flops=2 * flat_acts.size * FF,
        )

    other = swap(partial_of(True))
    mine = partial_of(False)
    whole, half = shape((FAR, PAIR, FF)), shape((FAR // 2, PAIR, FF))
    own, up1, up2, down2, down1 = call(
        add_kernel, (mine, other), [whole, whole, half, half, whole]
    )
    chunk = shape((PAIR, FF))
    arrived = (go(up2, 2), go(down2, -2), go(up1, 1), go(down1, -1))
    near = call(near_kernel, (own, *arrived), shape((FAR, PAIR, FF)))
    kept = lax.dynamic_index_in_dim(momentum, core, 1, keepdims=False)
    lent = swap(lax.dynamic_index_in_dim(momentum, 1 - core, 1, keepdims=False))
    rows = shape((ROWS, FF), F32)
    packed_rows = PACKED
    ns_input, new_mine, new_give, packed = call(
        momentum_kernel,
        (lax.all_to_all(near, "far", 0, 0), kept, lent),
        [chunk, rows, rows, shape((packed_rows, LANE))],
        flops=2 * PAIR * FF * FF,
    )
    packed = packed.reshape(NEAR, packed_rows // NEAR, LANE)
    near_parts = lax.all_to_all(packed, "near", 0, 0)
    near_sum = call(spread_sum_kernel, (near_parts,), shape(packed.shape))
    far_parts = lax.all_to_all(near_sum, "far", 0, 0)
    far_sum = call(spread_sum_kernel, (far_parts,), shape(packed.shape, F32))
    gram = lax.all_to_all(far_sum, "near", 0, 0).reshape(packed_rows, LANE)

    new_other = swap(new_give)
    new_momentum = jnp.stack(
        [jnp.where(core == 0, new_mine, new_other), jnp.where(core == 0, new_other, new_mine)], axis=1
    )

    owner_ids = packing[:, 0]
    experts = owner_ids.shape[0]
    positions = jnp.arange(experts, dtype=jnp.int32)
    shared = (owner_ids[:, None] == owner_ids[None, :]) & (positions[None, :] < positions[:, None])
    target = owner_ids * MOST + jnp.sum(shared.astype(jnp.int32), axis=1)
    of_core, of_y = positions % CORES, positions // CORES % n_y
    of_x = positions // (CORES * n_y)
    slots = jnp.arange(MOST, dtype=jnp.int32)
    line = (jnp.arange(n_x, dtype=jnp.int32)[:, None] * n_y + y) * MOST + slots[None, :]
    passes = (line.reshape(-1)[:, None] == target[None, :]) & (of_x == x)[None, :]
    placed_from = jnp.max(jnp.where(passes, (of_core * n_y + of_y)[None, :], -1), axis=1)
    fills = ((x * n_y + y) * MOST + slots)[:, None] == target[None, :]
    stacked_from = jnp.max(jnp.where(fills, of_x[None, :], -1), axis=1)
    my_owner = lax.dynamic_slice_in_dim(owner_ids, (x * n_y + y) * CORES + core, 1, 0)

    sent = call(
        newton_schulz_kernel,
        (my_owner, gram, ns_input),
        shape((CORES, n_y, ROWS, FF)),
        scalars=1,
        flops=2 * 27 * FF * FF * FF,
    )
    got = lax.all_to_all(sent.reshape(CORES * n_y, ROWS, FF), ("core", "y"), 0, 0)
    placed = call(place_kernel, (placed_from, got), shape((n_x, MOST, ROWS, FF)), scalars=1)
    got = lax.all_to_all(placed, "x", 0, 0)
    stacked = call(
        stack_kernel,
        (stacked_from, got),
        shape((ROWS, MOST, FF)),
        scalars=1,
        scratch=[pltpu.VMEM((ROWS, MOST, FF), F32)],
    )
    return new_momentum, stacked


def solution(mesh):
    devices = np.asarray(mesh.devices)
    side = math.isqrt(devices.shape[1])
    devices = devices.reshape(FAR, NEAR, CORES, side, side)
    finer = Mesh(devices, ("far", "near", "core", "x", "y"))
    spec = P(("far", "near", "core"), ("x", "y"), None)
    return jax.shard_map(
        body, mesh=finer, in_specs=(spec,) * 4 + (P(),), out_specs=(spec, spec), check_vma=False
    )
```

```python
import functools
import math

import jax
import jax.numpy as jnp
import numpy as np
from jax import lax
from jax.experimental import pallas as pl
from jax.experimental.pallas import tpu as pltpu
from jax.sharding import Mesh
from jax.sharding import PartitionSpec as P

D = 2048
FF = 384
TILE = 256
ITERS = 3
MOST = 4
CORES = 2
NEAR = 4
FAR = 4
ROWS = 64
PAIR = CORES * ROWS
LANE = 128

COEF_A = 3.4445
COEF_B = -4.775
COEF_C = 2.0315
BETA = 0.95
EPSILON = 1e-07
BLOCKS = ((0, 1), (0, 2), (1, 2))
SIDE = FF // LANE
HALF = LANE // 2
PACKED = len(BLOCKS) * LANE + (SIDE + 2) * HALF
MIB = 1024 * 1024
VMEM = pl.BlockSpec(memory_space=pltpu.VMEM)
SMEM = pl.BlockSpec(memory_space=pltpu.SMEM)
BF16 = jnp.bfloat16
F32 = jnp.float32


def call(kernel, args, outs, scalars=0, scratch=(), flops=0):
    many = isinstance(outs, list)
    nbytes = sum(a.size * a.dtype.itemsize for a in args)
    return pl.pallas_call(
        kernel,
        out_shape=outs,
        in_specs=[SMEM] * scalars + [VMEM] * (len(args) - scalars),
        out_specs=[VMEM] * len(outs) if many else VMEM,
        scratch_shapes=list(scratch),
        compiler_params=pltpu.CompilerParams(vmem_limit_bytes=16 * MIB),
        cost_estimate=pl.CostEstimate(flops=flops, bytes_accessed=nbytes, transcendentals=0),
    )(*args)


def shape(dims, dtype=BF16):
    return jax.ShapeDtypeStruct(dims, dtype)


def transposed_dot(x, y):
    return lax.dot_general(x, y, (((0,), (0,)), ((), ())), preferred_element_type=F32)


def masked_grads(expert, ids_ref, grads_ref, masked_ref):
    for tile in range(grads_ref.shape[0] // TILE):
        rows = slice(tile * TILE, (tile + 1) * TILE)
        factor = jnp.where(ids_ref[tile] == expert, 1.0, 0.0).astype(F32)
        masked_ref[rows, :] = (grads_ref[rows, :].astype(F32) * factor).astype(BF16)
    return masked_ref[...]


def chunk_rows(q, rel):
    at = lax.rem(lax.axis_index("near") + rel, NEAR)
    return pl.ds(pl.multiple_of((q * NEAR + at) * PAIR, PAIR), PAIR)


def partial_kernel(theirs, ids_ref, acts_ref, grads_ref, out_ref, masked_ref):
    core = lax.axis_index("core")
    masked = masked_grads(1 - core if theirs else core, ids_ref, grads_ref, masked_ref)
    for rel in range(NEAR):
        for q in range(FAR):
            block = transposed_dot(acts_ref[:, chunk_rows(q, rel)], masked)
            out_ref[rel, q] = block.astype(BF16)


def add_kernel(mine_ref, other_ref, own_ref, up1_ref, up2_ref, down2_ref, down1_ref):
    def total(rel, qs):
        return (mine_ref[rel, qs].astype(F32) + other_ref[rel, qs].astype(F32)).astype(BF16)

    half = FAR // 2
    own_ref[...] = total(0, slice(None))
    up1_ref[...] = total(1, slice(None))
    up2_ref[...] = total(2, slice(0, half))
    down2_ref[...] = total(2, slice(half, FAR))
    down1_ref[...] = total(3, slice(None))


def near_kernel(own_ref, c_ref, d_ref, a_ref, b_ref, out_ref):
    half = FAR // 2
    for q in range(FAR):
        last = c_ref[q] if q < half else d_ref[q - half]
        total = own_ref[q].astype(F32) + a_ref[q].astype(F32)
        out_ref[q] = (total + (b_ref[q].astype(F32) + last.astype(F32))).astype(BF16)


def momentum_kernel(
    parts_ref, kept_ref, lent_ref, ns_ref, mine_ref, give_ref, gram_ref
):
    core = lax.axis_index("core")
    for who, old_ref, new_ref in ((core, kept_ref, mine_ref), (1 - core, lent_ref, give_ref)):
        rows = pl.ds(pl.multiple_of(who * ROWS, ROWS), ROWS)
        grad = parts_ref[0, rows, :].astype(F32)
        for at in range(1, FAR):
            grad = grad + parts_ref[at, rows, :].astype(F32)
        new = BETA * old_ref[...] + grad
        new_ref[...] = new
        ns_ref[rows, :] = (grad + BETA * new).astype(BF16)
    x = ns_ref[...]
    gram = transposed_dot(x, x)
    top, bottom = [], []
    for i in range(SIDE):
        columns = slice(i * LANE, (i + 1) * LANE)
        top.append(gram[i * LANE : i * LANE + HALF, columns])
        bottom.append(gram[i * LANE + HALF : (i + 1) * LANE, columns])
    left = lax.broadcasted_iota(jnp.int32, (HALF, LANE), 1) < HALF
    pair = jnp.where(left, pltpu.roll(bottom[0], HALF, 1), bottom[1])
    whole = [gram[i * LANE : (i + 1) * LANE, j * LANE : (j + 1) * LANE] for i, j in BLOCKS]
    at = 0
    for part in whole + top + [pair, bottom[2]]:
        gram_ref[at : at + part.shape[0], :] = part.astype(BF16)
        at += part.shape[0]


def spread_sum_kernel(parts_ref, out_ref):
    total = parts_ref[0].astype(F32)
    for at in range(1, parts_ref.shape[0]):
        total = total + parts_ref[at].astype(F32)
    for at in range(out_ref.shape[0]):
        out_ref[at] = total.astype(out_ref.dtype)


def split(x):
    high = x.astype(BF16)
    return high, (x - high.astype(F32)).astype(BF16)


def dot(x, y):
    return jnp.dot(x, y, preferred_element_type=F32)


def dot3(x, y):
    (xh, xl), (yh, yl) = x, y
    return dot(jnp.concatenate([xh, xl, xh], axis=1), jnp.concatenate([yh, yh, yl], axis=0))


def square3(x):
    high, low = x
    mixed = dot(high, low)
    return dot(high, high) + (mixed + mixed.T)


def newton_schulz_kernel(owner_ref, gram_ref, x_ref, out_ref):
    blocks = {}
    for at, (i, j) in enumerate(BLOCKS):
        block = gram_ref[at * LANE : (at + 1) * LANE, :]
        blocks[i, j], blocks[j, i] = block, block.T
    start = len(BLOCKS) * LANE
    halves = [gram_ref[start + i * HALF : start + (i + 1) * HALF, :] for i in range(SIDE + 2)]
    left = lax.broadcasted_iota(jnp.int32, (HALF, LANE), 1) < HALF
    corners = (pltpu.roll(halves[SIDE], HALF, 1), halves[SIDE], halves[SIDE + 1])
    for i in range(SIDE):
        turned = jnp.concatenate([halves[i], halves[i]], axis=0).T
        below = jnp.where(left, turned[HALF:, :], corners[i])
        blocks[i, i] = jnp.concatenate([halves[i], below], axis=0)
    gram = jnp.concatenate(
        [jnp.concatenate([blocks[i, j] for j in range(3)], axis=1) for i in range(3)], axis=0
    )
    rows = lax.broadcasted_iota(jnp.int32, (FF, FF), 0)
    cols = lax.broadcasted_iota(jnp.int32, (FF, FF), 1)
    eye = (rows == cols).astype(F32)
    trace = jnp.sum(jnp.sum(gram * eye, axis=1, keepdims=True), axis=0, keepdims=True)
    inv_norm = 1.0 / (jnp.sqrt(trace) + EPSILON)
    weights = gram * (inv_norm * inv_norm)
    current = x_ref[...].astype(F32) * inv_norm
    for sweep in range(ITERS):
        parts = split(weights)
        poly = COEF_A * eye + COEF_B * weights + COEF_C * square3(parts)
        poly_parts = split(poly)
        current = dot3(split(current), poly_parts)
        if sweep < ITERS - 1:
            weights = dot3(split(dot3(parts, poly_parts)), poly_parts)
    update = (current * math.sqrt(D)).astype(BF16)
    out_ref[...] = jnp.zeros_like(out_ref)
    for core in range(CORES):
        out_ref[core, lax.rem(owner_ref[0], out_ref.shape[1])] = update[core * ROWS : (core + 1) * ROWS, :]


def place_kernel(source_ref, got_ref, out_ref):
    out_ref[...] = jnp.zeros_like(out_ref)
    for owner in range(out_ref.shape[0]):
        for slot in range(MOST):
            source = source_ref[owner * MOST + slot]

            @pl.when(source >= 0)
            def _():
                out_ref[owner, slot] = got_ref[source]


def stack_kernel(source_ref, got_ref, out_ref, wide_ref):
    for slot in range(MOST):
        source = source_ref[slot]
        filled = jnp.where(source >= 0, 1.0, 0.0).astype(F32)
        wide_ref[:, slot, :] = got_ref[jnp.maximum(source, 0), slot].astype(F32) * filled
    out_ref[...] = wide_ref[...].astype(BF16)


def ring(size, step):
    return [(i, (i + step) % size) for i in range(size)]


def body(acts, grads, tile_expert, momentum, packing):
    core, x, y = (lax.axis_index(name) for name in ("core", "x", "y"))
    n_x, n_y = lax.axis_size("x"), lax.axis_size("y")
    flat_acts, flat_grads = acts[:, 0, :], grads[:, 0, :]

    def go(value, step):
        return lax.ppermute(value, ("far", "near"), ring(FAR * NEAR, step))

    def swap(value):
        return lax.ppermute(value, "core", ring(CORES, 1))

    def partial_of(theirs):
        return call(
            functools.partial(partial_kernel, theirs),
            (tile_expert[:, 0, 0], flat_acts, flat_grads),
            shape((NEAR, FAR, PAIR, FF)),
            scalars=1,
            scratch=[pltpu.VMEM(flat_grads.shape, BF16)],
            flops=2 * flat_acts.size * FF,
        )

    other = swap(partial_of(True))
    mine = partial_of(False)
    whole, half = shape((FAR, PAIR, FF)), shape((FAR // 2, PAIR, FF))
    own, up1, up2, down2, down1 = call(
        add_kernel, (mine, other), [whole, whole, half, half, whole]
    )
    chunk = shape((PAIR, FF))
    arrived = (go(up2, 2), go(down2, -2), go(up1, 1), go(down1, -1))
    near = call(near_kernel, (own, *arrived), shape((FAR, PAIR, FF)))
    kept = lax.dynamic_index_in_dim(momentum, core, 1, keepdims=False)
    lent = swap(lax.dynamic_index_in_dim(momentum, 1 - core, 1, keepdims=False))
    rows = shape((ROWS, FF), F32)
    packed_rows = PACKED
    ns_input, new_mine, new_give, packed = call(
        momentum_kernel,
        (lax.all_to_all(near, "far", 0, 0), kept, lent),
        [chunk, rows, rows, shape((packed_rows, LANE))],
        flops=2 * PAIR * FF * FF,
    )
    packed = packed.reshape(NEAR, packed_rows // NEAR, LANE)
    near_parts = lax.all_to_all(packed, "near", 0, 0)
    near_sum = call(spread_sum_kernel, (near_parts,), shape(packed.shape))
    far_parts = lax.all_to_all(near_sum, "far", 0, 0)
    far_sum = call(spread_sum_kernel, (far_parts,), shape(packed.shape, F32))
    gram = lax.all_to_all(far_sum, "near", 0, 0).reshape(packed_rows, LANE)

    new_other = swap(new_give)
    new_momentum = jnp.stack(
        [jnp.where(core == 0, new_mine, new_other), jnp.where(core == 0, new_other, new_mine)], axis=1
    )

    owner_ids = packing[:, 0]
    experts = owner_ids.shape[0]
    positions = jnp.arange(experts, dtype=jnp.int32)
    shared = (owner_ids[:, None] == owner_ids[None, :]) & (positions[None, :] < positions[:, None])
    target = owner_ids * MOST + jnp.sum(shared.astype(jnp.int32), axis=1)
    of_core, of_y = positions % CORES, positions // CORES % n_y
    of_x = positions // (CORES * n_y)
    slots = jnp.arange(MOST, dtype=jnp.int32)
    line = (jnp.arange(n_x, dtype=jnp.int32)[:, None] * n_y + y) * MOST + slots[None, :]
    passes = (line.reshape(-1)[:, None] == target[None, :]) & (of_x == x)[None, :]
    placed_from = jnp.max(jnp.where(passes, (of_core * n_y + of_y)[None, :], -1), axis=1)
    fills = ((x * n_y + y) * MOST + slots)[:, None] == target[None, :]
    stacked_from = jnp.max(jnp.where(fills, of_x[None, :], -1), axis=1)
    my_owner = lax.dynamic_slice_in_dim(owner_ids, (x * n_y + y) * CORES + core, 1, 0)

    sent = call(
        newton_schulz_kernel,
        (my_owner, gram, ns_input),
        shape((CORES, n_y, ROWS, FF)),
        scalars=1,
        flops=2 * 27 * FF * FF * FF,
    )
    got = lax.all_to_all(sent.reshape(CORES * n_y, ROWS, FF), ("core", "y"), 0, 0)
    placed = call(place_kernel, (placed_from, got), shape((n_x, MOST, ROWS, FF)), scalars=1)
    got = lax.all_to_all(placed, "x", 0, 0)
    stacked = call(
        stack_kernel,
        (stacked_from, got),
        shape((ROWS, MOST, FF)),
        scalars=1,
        scratch=[pltpu.VMEM((ROWS, MOST, FF), F32)],
    )
    return new_momentum, stacked


def solution(mesh):
    devices = np.asarray(mesh.devices)
    side = math.isqrt(devices.shape[1])
    devices = devices.reshape(FAR, NEAR, CORES, side, side)
    finer = Mesh(devices, ("far", "near", "core", "x", "y"))
    spec = P(("far", "near", "core"), ("x", "y"), None)
    return jax.shard_map(
        body, mesh=finer, in_specs=(spec,) * 4 + (P(),), out_specs=(spec, spec), check_vma=False
    )
```
